32 devices in a mesh: rep: 4 (over x, core), shard: 8 (over z, y).
Axes of the slice: x: 2, y: 2, z: 4, core: 2. Of those that a mesh axis runs over, the one named last changes fastest.
Arguments:
- tokens: bfloat16 [16384, 1024], P(('rep', 'shard')), may hold values from -6 to 6
- cotangent: bfloat16 [16384, 1024], P(('rep', 'shard')), may hold values from -6 to 6
- lengths: int32 [32, 4], P(('rep', 'shard')), may hold values from 0 to 512, as said below
- joint_weight: bfloat16 [1024, 3072], P('shard'), may hold values from -0.1875 to 0.1875
- query_bias: bfloat16 [1024], P('shard'), may hold values from -3 to 3
- value_bias: bfloat16 [1024], P('shard'), may hold values from -3 to 3
- output_weight: bfloat16 [1024, 1024], P('shard'), may hold values from -0.75 to 0.75
- output_bias: bfloat16 [1024], P('shard'), may hold values from -3 to 3
- norm_gain: bfloat16 [1024], P('shard'), may hold values from 0.5 to 1.5
- norm_shift: bfloat16 [1024], P('shard'), may hold values from -3 to 3
- expand_weight: bfloat16 [1024, 4096], P('shard'), may hold values from -0.1875 to 0.1875
- expand_bias: bfloat16 [4096], P('shard'), may hold values from -3 to 3
- reduce_weight: bfloat16 [4096, 1024], P('shard'), may hold values from -0.09375 to 0.09375
- reduce_bias: bfloat16 [1024], P('shard'), may hold values from -3 to 3
- final_gain: bfloat16 [1024], P('shard'), may hold values from 0.5 to 1.5
- final_shift: bfloat16 [1024], P('shard'), may hold values from -3 to 3
Outputs:
- output: bfloat16 [16384, 1024], P(('rep', 'shard'))
- grad_tokens: bfloat16 [16384, 1024], P(('rep', 'shard'))
- grad_joint_weight: float32 [1024, 3072], P('shard')
- grad_query_bias: float32 [1024], P('shard')
- grad_value_bias: float32 [1024], P('shard')
- grad_output_weight: float32 [1024, 1024], P('shard')
- grad_output_bias: float32 [1024], P('shard')
- grad_norm_gain: float32 [1024], P('shard')
- grad_norm_shift: float32 [1024], P('shard')
- grad_expand_weight: float32 [1024, 4096], P('shard')
- grad_expand_bias: float32 [4096], P('shard')
- grad_reduce_weight: float32 [4096, 1024], P('shard')
- grad_reduce_bias: float32 [1024], P('shard')
- grad_final_gain: float32 [1024], P('shard')
- grad_final_shift: float32 [1024], P('shard')
The draws below stay inside these ranges and needn't reach their ends.
Inputs may be any that keep to these rules, and one draw needn't show every extreme that they name: `lengths`: each row sums to between 256 and 512; slots past the sum are padding; in every draw one row holds a single sequence of 512 tokens.
All inputs are finite; a program needn't handle non-finite values.
Results may differ from the reference program's by a relative error of at most 0.013.
Values may be sent and summed in bfloat16 or wider, within the bound.
A program may use at most 192 MiB of HBM per device.

```python
import jax
import jax.numpy as jnp
from jax import lax

D = 1024
FF = 4096
HEADS = 16
HEAD_DIM = 64
TOK_DEV = 512
SEQ_DEV = 4
TOKENS = 16384
N_REP = 4
N_SHARD = 8


def draw_lengths(key, part):
    key = jax.random.fold_in(key, 11)
    total_key, cut_key, full_key = jax.random.split(key, 3)
    row_count = N_REP * N_SHARD
    totals = jax.random.randint(total_key, (row_count, 1), TOK_DEV // 2, TOK_DEV + 1).astype(jnp.int32)
    cut_points = jnp.sort(jax.random.randint(cut_key, (row_count, SEQ_DEV - 1), 0, TOK_DEV + 1).astype(jnp.int32), axis=1)
    cut_points = cut_points * totals // TOK_DEV
    edge_points = jnp.concatenate([jnp.zeros((row_count, 1), jnp.int32), cut_points, totals], axis=1)
    span_lengths = edge_points[:, 1:] - edge_points[:, :-1]
    chosen = jax.random.randint(full_key, (), 0, row_count)
    single = jnp.concatenate([jnp.full((1,), TOK_DEV, jnp.int32), jnp.zeros((SEQ_DEV - 1,), jnp.int32)])
    picked = (jnp.arange(row_count) == chosen)[:, None]
    return jnp.where(picked, single[None, :], span_lengths).astype(jnp.int32)


def spiked(array, own_key, source, target, shards_of, factor):
    owner, partner = [(jnp.arange(array.shape[dim]) // (array.shape[dim] // shards_of)).reshape([-1 if axis == dim else 1 for axis in range(array.ndim)]) for dim in (source, target)]
    chosen = jax.random.permutation(own_key, shards_of)[partner]
    strong = (owner == chosen) | (owner == (partner + shards_of // 2) % shards_of)
    return jnp.where(strong, factor * array, array)


def level_of(stream_key, extent, pieces, smallest, top_value):
    factor_of, own = 1.0, jax.random.fold_in(stream_key, 6)
    for dim, blocks in pieces:
        steps = jnp.exp(jax.random.uniform(jax.random.fold_in(own, dim), (blocks,), jnp.float32, smallest / len(pieces), top_value / len(pieces)))
        factor_of = factor_of * jnp.repeat(steps, extent[dim] // blocks).reshape([-1 if axis == dim else 1 for axis in range(len(extent))])
    return factor_of


def noise(stream_key, extent, width, reach, pieces=(), kind=jnp.bfloat16):
    factor_of = level_of(stream_key, extent, pieces, -0.22, 0.18) if pieces else 1.0
    array = jax.random.normal(stream_key, extent, jnp.float32) * width * factor_of
    return jnp.minimum(jnp.maximum(array, -reach), reach).astype(kind)


def heavy_noise(rng, shape, width, limit, pieces, heavy, held_as=jnp.bfloat16):
    result = width * jax.random.normal(rng, shape, jnp.float32)
    if pieces:
        result = result * level_of(rng, shape, pieces, -0.22, 0.18)
    return jnp.clip(spiked(result, jax.random.fold_in(rng, 3), *heavy), -limit, limit).astype(held_as)


def setup_inputs(seed: int = 0) -> dict:
    arg_keys = jax.random.split(jax.random.key(seed), 17)
    tokens = noise(arg_keys[0], (TOKENS, D), 1.0, 6.0, ((0, 32),))
    cotangent = heavy_noise(arg_keys[1], (TOKENS, D), 1.0, 6.0, ((0, 32),), (0, 1, 32, 2.75))
    lengths = draw_lengths(jax.random.fold_in(arg_keys[16], 71), 0)
    joint_weight = noise(arg_keys[3], (D, 3 * D), D ** -0.5, 0.1875, ((0, 8),))
    query_bias = noise(arg_keys[4], (D,), 0.5, 3.0, ((0, 8),))
    value_bias = noise(arg_keys[5], (D,), 0.5, 3.0, ((0, 8),))
    output_weight = noise(arg_keys[6], (D, D), (D // 16) ** -0.5, 0.75, ((0, 8),))
    output_bias = noise(arg_keys[7], (D,), 0.5, 3.0, ((0, 8),))
    norm_gain = jnp.clip(1.0 + 0.1 * jax.random.normal(arg_keys[8], (D,), jnp.float32), 0.5, 1.5).astype(jnp.bfloat16)
    norm_shift = noise(arg_keys[9], (D,), 0.5, 3.0, ((0, 8),))
    expand_weight = noise(arg_keys[10], (D, FF), D ** -0.5, 0.1875, ((0, 8),))
    expand_bias = noise(arg_keys[11], (FF,), 0.5, 3.0, ((0, 8),))
    reduce_weight = noise(arg_keys[12], (FF, D), FF ** -0.5, 0.09375, ((0, 8),))
    reduce_bias = noise(arg_keys[13], (D,), 0.5, 3.0, ((0, 8),))
    final_gain = jnp.clip(1.0 + 0.1 * jax.random.normal(arg_keys[14], (D,), jnp.float32), 0.5, 1.5).astype(jnp.bfloat16)
    final_shift = noise(arg_keys[15], (D,), 0.5, 3.0, ((0, 8),))
    return dict(tokens=tokens, cotangent=cotangent, lengths=lengths, joint_weight=joint_weight, query_bias=query_bias, value_bias=value_bias, output_weight=output_weight, output_bias=output_bias, norm_gain=norm_gain, norm_shift=norm_shift, expand_weight=expand_weight, expand_bias=expand_bias, reduce_weight=reduce_weight, reduce_bias=reduce_bias, final_gain=final_gain, final_shift=final_shift)


@jax.custom_vjp
def low(v):
    return lax.optimization_barrier(v.astype(jnp.bfloat16)).astype(jnp.float32)

@jax.custom_vjp
def low_back(v):
    return v

def low_keep(v):
    return (low(v), None)

def low_pass(kept, grad):
    return (grad,)

def back_keep(v):
    return (v, None)

def back_low(kept, grad):
    return (low(grad),)
low.defvjp(low_keep, low_pass)
low_back.defvjp(back_keep, back_low)
epsilon = 1e-05
mask_fill = -1000000000.0
highest = lax.Precision.HIGHEST

def matmul(left_side, right_side):
    return jnp.dot(left_side, right_side, precision=highest)

def layer_norm(inputs, gain_vector, shift_vector):
    centre = inputs - lax.optimization_barrier(jnp.mean(inputs, axis=-1, keepdims=True))
    variance = lax.optimization_barrier(jnp.mean(centre * centre, axis=-1, keepdims=True))
    return centre * lax.rsqrt(variance + epsilon) * gain_vector + shift_vector

def gelu_exact(inputs):
    return 0.5 * inputs * (1.0 + jax.scipy.special.erf(inputs * 0.7071067811865476))

def segment_of(length_row, row_count):
    seq_ends = jnp.cumsum(length_row.astype(jnp.int32)).astype(jnp.int32)
    position = jnp.arange(row_count, dtype=jnp.int32)
    return lax.optimization_barrier(jnp.sum((position[:, None] >= seq_ends[None, :]).astype(jnp.int32), axis=1)).astype(jnp.int32)

def attention(queries, key_rows, values, segment):
    row_count = queries.shape[0]
    block_size = min(512, row_count)
    score_scale = HEAD_DIM ** (-0.5)
    key_heads = key_rows.reshape(row_count, HEADS, HEAD_DIM)
    value_heads = values.reshape(row_count, HEADS, HEAD_DIM)

    def one_block(block_args):
        query_block, segment_block = block_args
        scores = jnp.einsum('qhd,khd->hqk', query_block, key_heads, precision=highest) * score_scale
        scores = low_back(scores)
        scores = jnp.where((segment_block[:, None] == segment[None, :])[None], scores, mask_fill)
        row_max = lax.optimization_barrier(jnp.max(scores, axis=-1, keepdims=True))
        powers = jnp.exp(scores - row_max)
        attn_weights = low(powers / lax.optimization_barrier(jnp.sum(powers, axis=-1, keepdims=True)))
        context = jnp.einsum('hqk,khd->qhd', attn_weights, value_heads, precision=highest)
        return context.reshape(block_size, D)
    blocks = lax.map(jax.checkpoint(one_block), (queries.reshape(row_count // block_size, block_size, HEADS, HEAD_DIM), segment.reshape(row_count // block_size, block_size)))
    return blocks.reshape(row_count, D)

def block_forward(x_block, length_row, params):
    joint_weight, query_bias, value_bias, output_weight, output_bias, norm_gain, norm_shift, expand_weight, expand_bias, reduce_weight, reduce_bias, final_gain, final_shift = params
    segment = segment_of(length_row, TOK_DEV)
    live_rows = (segment < SEQ_DEV).astype(jnp.float32)
    joint = matmul(x_block, joint_weight)
    queries = low(low_back(joint[:, :D] + query_bias))
    key_rows = low(low_back(joint[:, D:2 * D]))
    values = low(low_back(joint[:, 2 * D:] + value_bias))
    context = low(low_back(attention(queries, key_rows, values, segment)))
    branch = low_back(matmul(context, output_weight) + output_bias)
    middle = layer_norm(x_block + branch, norm_gain, norm_shift)
    hidden = low_back(matmul(low(middle), expand_weight) + expand_bias)
    active = low(gelu_exact(hidden))
    second = low_back(matmul(active, reduce_weight) + reduce_bias)
    return layer_norm(middle + second, final_gain, final_shift) * live_rows[:, None]

def reference(tokens, cotangent, lengths, joint_weight, query_bias, value_bias, output_weight, output_bias, norm_gain, norm_shift, expand_weight, expand_bias, reduce_weight, reduce_bias, final_gain, final_shift):
    params = tuple((param.astype(jnp.float32) for param in (joint_weight, query_bias, value_bias, output_weight, output_bias, norm_gain, norm_shift, expand_weight, expand_bias, reduce_weight, reduce_bias, final_gain, final_shift)))
    block_count = lengths.shape[0]
    token_blocks = tokens.astype(jnp.float32).reshape(block_count, TOK_DEV, D)

    def forward(token_input, param_input):

        def step(state_carry, item):
            x_block, length_row = item
            return (state_carry, jax.checkpoint(block_forward)(x_block, length_row, param_input))
        _, outputs = lax.scan(step, jnp.float32(0.0), (token_input, lengths))
        return outputs
    output, pullback = jax.vjp(forward, token_blocks, params)
    grad_blocks, grads = pullback(cotangent.astype(jnp.float32).reshape(block_count, TOK_DEV, D))
    return (output.reshape(block_count * TOK_DEV, D).astype(jnp.bfloat16), grad_blocks.reshape(block_count * TOK_DEV, D).astype(jnp.bfloat16), grads[0], grads[1], grads[2], grads[3], grads[4], grads[5], grads[6], grads[7], grads[8], grads[9], grads[10], grads[11], grads[12])
```

```python
import functools

import jax
import jax.numpy as jnp
from jax import lax
from jax.sharding import PartitionSpec as P

HEADS = 16


epsilon = 1e-05
mask_fill = -1000000000.0


def layer_norm(inputs, gain_vector, shift_vector):
    centre = inputs - jnp.mean(inputs, axis=-1, keepdims=True)
    variance = jnp.mean(centre * centre, axis=-1, keepdims=True)
    return centre * lax.rsqrt(variance + epsilon) * gain_vector + shift_vector


def gelu_exact(inputs):
    return 0.5 * inputs * (1.0 + jax.scipy.special.erf(inputs * 0.7071067811865476))


def segment_of(length_row, row_count):
    seq_ends = jnp.cumsum(length_row)
    position = jnp.arange(row_count, dtype=jnp.int32)
    return jnp.sum((position[:, None] >= seq_ends[None, :]).astype(jnp.int32), axis=1)


def block_scores(query_block, key_heads, segment_block, segment, score_scale):
    scores = (
        jnp.einsum("qhd,khd->hqk", query_block, key_heads, preferred_element_type=jnp.float32)
        * score_scale
    )
    return jnp.where((segment_block[:, None] == segment[None, :])[None], scores, mask_fill)


def attend_forward(queries, key_rows, values, segment, head_count):
    row_count, model_width = queries.shape
    head_size = model_width // head_count
    block_size = min(512, row_count)
    score_scale = head_size ** (-0.5)
    key_heads = key_rows.reshape(row_count, head_count, head_size)
    value_heads = values.reshape(row_count, head_count, head_size)

    def one_block(state_carry, block_index):
        query_block = queries.reshape(block_size, head_count, head_size)
        scores = block_scores(query_block, key_heads, segment, segment, score_scale)
        row_max = jnp.max(scores, axis=-1, keepdims=True)
        powers = jnp.exp(scores - row_max)
        row_total = jnp.sum(powers, axis=-1, keepdims=True)
        attn_weights = (powers / row_total).astype(jnp.bfloat16)
        context = jnp.einsum(
            "hqk,khd->qhd", attn_weights, value_heads, preferred_element_type=jnp.float32
        )
        log_total = (row_max + jnp.log(row_total))[..., 0]
        return (
            state_carry,
            (context.reshape(block_size, model_width).astype(jnp.bfloat16), log_total),
        )

    _, (context, log_total) = lax.scan(one_block, 0, jnp.arange(row_count // block_size))
    return (context.reshape(row_count, model_width), log_total)


def attend_backward(queries, key_rows, values, segment, log_total, grad_context, head_count):
    row_count, model_width = queries.shape
    head_size = model_width // head_count
    block_size = min(512, row_count)
    score_scale = head_size ** (-0.5)
    key_heads = key_rows.reshape(row_count, head_count, head_size)
    value_heads = values.reshape(row_count, head_count, head_size)

    def one_block(state_carry, block_items):
        grad_keys, grad_values = state_carry
        block_index, block_total = block_items
        query_block = queries.reshape(block_size, head_count, head_size)
        grad_block = grad_context.reshape(block_size, head_count, head_size)
        scores = block_scores(query_block, key_heads, segment, segment, score_scale)
        attn_weights = jnp.exp(scores - block_total[..., None])
        grad_weights = jnp.einsum(
            "qhd,khd->hqk", grad_block, value_heads, preferred_element_type=jnp.float32
        )
        inner = jnp.sum(attn_weights * grad_weights, axis=-1, keepdims=True)
        grad_scores = (attn_weights * (grad_weights - inner)).astype(jnp.bfloat16)
        grad_query = (
            jnp.einsum("hqk,khd->qhd", grad_scores, key_heads, preferred_element_type=jnp.float32)
            * score_scale
        )
        grad_keys = (
            grad_keys
            + jnp.einsum(
                "hqk,qhd->khd", grad_scores, query_block, preferred_element_type=jnp.float32
            )
            * score_scale
        )
        grad_values = grad_values + jnp.einsum(
            "hqk,qhd->khd",
            attn_weights.astype(jnp.bfloat16),
            grad_block,
            preferred_element_type=jnp.float32,
        )
        return ((grad_keys, grad_values), grad_query.reshape(block_size, model_width))

    zero_heads = jnp.zeros((row_count, head_count, head_size), jnp.float32)
    (grad_keys, grad_values), grad_queries = lax.scan(
        one_block, (zero_heads, zero_heads), (jnp.arange(row_count // block_size), log_total)
    )
    return (
        grad_queries.reshape(row_count, model_width),
        grad_keys.reshape(row_count, model_width),
        grad_values.reshape(row_count, model_width),
    )


def flip_pairs(rep_count, shard_count, rep_bit, shard_bit):
    pairs = []
    for rep in range(rep_count):
        for shard in range(shard_count):
            to_rep = rep ^ rep_bit[rep % 2]
            to_shard = shard ^ shard_bit[rep % 2]
            pairs.append((rep * shard_count + shard, to_rep * shard_count + to_shard))
    return pairs


class Links:
    def __init__(self, mesh):
        rep_count, shard_count = mesh.shape["rep"], mesh.shape["shard"]
        self.rep_count, self.shard_count = rep_count, shard_count
        self.shard_bits = shard_count.bit_length() - 1

        def pairs(rep_bit, shard_bit):
            return flip_pairs(rep_count, shard_count, rep_bit, shard_bit)

        self.core = pairs((1, 1), (0, 0))
        self.x = pairs((2, 2), (0, 0))
        self.first = pairs((2, 0), (0, 1))
        self.second = pairs((0, 2), (1, 0))
        self.bits = [pairs((0, 0), (1 << b, 1 << b)) for b in range(self.shard_bits)]

    def send(self, array, pairs):
        return lax.ppermute(array, ("rep", "shard"), pairs)


def after(array, marker):
    if marker is None:
        return array
    return lax.optimization_barrier((array, marker))[0]


def take(array, index, axis):
    return lax.dynamic_index_in_dim(array, index, axis, keepdims=False)


def put_pair(mine, other, bit, axis):
    return jnp.where(bit == 0, jnp.stack([mine, other], axis), jnp.stack([other, mine], axis))


def place():
    rep, shard = lax.axis_index("rep"), lax.axis_index("shard")
    return rep % 2, rep // 2, shard


def gather_weight(links, own, marks):
    core, x, shard = place()
    rows, width = own.shape
    quarter = rows // 4
    piece = take(take(own.reshape(2, 2, quarter, width), x, 0), core, 0)
    new_marks = []
    high = links.shard_bits - 1
    step = 0

    def mark_of(i):
        return marks[i] if marks else None

    part = piece[None]
    for b in range(high, 0, -1):
        got = links.send(after(part, mark_of(step)), links.bits[b])
        new_marks.append(got)
        bit = (shard >> b) % 2
        part = put_pair(part, got, bit, 1)
        part = part.reshape(-1, quarter, width)
        step += 1
    y = shard % 2
    final_q = y * 2 + x
    final = part
    mid = links.send(after(final, mark_of(step)), links.second)
    new_marks.append(mid)
    step += 1
    other_final = links.send(after(final, mark_of(step)), links.first)
    other_mid = links.send(mid, links.first)
    new_marks.append(other_mid)
    step += 1
    mid_q = jnp.where(core == 0, final_q ^ 2, final_q ^ 1)
    of_q = jnp.where(core == 0, final_q ^ 1, final_q ^ 2)
    om_q = 3 - final_q
    pieces = [final, mid, other_final, other_mid]
    far = [links.send(piece, links.core) for piece in pieces]
    whole = jnp.zeros((part.shape[0], 4, 2, quarter, width), own.dtype)
    zero = jnp.int32(0)
    for block, q in zip(pieces, (final_q, mid_q, of_q, om_q)):
        whole = lax.dynamic_update_slice(
            whole, block[:, None, None], (zero, q, core, zero, zero)
        )
    for block, q in zip(far, (final_q, of_q, mid_q, om_q)):
        whole = lax.dynamic_update_slice(
            whole, block[:, None, None], (zero, q, 1 - core, zero, zero)
        )
    return whole.reshape(rows * links.shard_count, width), new_marks


def add_low(mine, got):
    return (mine.astype(jnp.float32) + got.astype(jnp.float32)).astype(jnp.bfloat16)


def reduce_weight_grad(links, grad, marks):
    core, x, shard = place()
    total_rows, width = grad.shape
    rows = total_rows // links.shard_count
    quarter = rows // 4
    lead = links.shard_count // 2
    y = shard % 2
    view = grad.reshape(lead, 4, 2, quarter, width)
    final_q = y * 2 + x
    new_marks = []

    def mark_of(i):
        return marks[i] if marks else None

    mid_q = jnp.where(core == 0, final_q ^ 2, final_q ^ 1)
    of_q = jnp.where(core == 0, final_q ^ 1, final_q ^ 2)
    om_q = 3 - final_q
    order = (om_q, mid_q, of_q, final_q)
    far_order = (om_q, of_q, mid_q, final_q)

    def piece_of(q, c):
        zero = jnp.int32(0)
        block = lax.dynamic_slice(view, (zero, q, c, zero, zero), (lead, 1, 1, quarter, width))
        return block.reshape(lead, quarter, width)

    sums = []
    for q, far_q in zip(order, far_order):
        got = links.send(after(piece_of(far_q, 1 - core), mark_of(0)), links.core)
        sums.append(add_low(piece_of(q, core), got))
    new_marks.append(got)
    send_mid, mid, send_final, final = sums
    got_mid = links.send(after(send_mid, mark_of(1)), links.first)
    mid = add_low(mid, got_mid)
    got_final = links.send(after(send_final, got_mid), links.first)
    new_marks.append(got_final)
    got = links.send(after(mid, mark_of(2)), links.second)
    new_marks.append(got)
    total = (final.astype(jnp.float32) + got_final.astype(jnp.float32) + got.astype(jnp.float32)).astype(
        jnp.bfloat16
    )
    step = 3
    for b in range(1, links.shard_bits):
        bit = (shard >> b) % 2
        pairs = total.reshape(-1, 2, quarter, width)
        got = links.send(after(take(pairs, 1 - bit, 1), mark_of(step)), links.bits[b])
        new_marks.append(got)
        total = add_low(take(pairs, bit, 1), got)
        step += 1
    total = total.reshape(quarter, width)
    both_x = put_pair(total, links.send(after(total, mark_of(step)), links.x), x, 0)
    new_marks.append(both_x)
    both = put_pair(both_x, links.send(both_x, links.core), core, 1)
    return both.reshape(rows, width).astype(jnp.float32), new_marks


def gather_small(links, own):
    _, _, shard = place()
    part = own[None]
    for b in range(links.shard_bits):
        got = links.send(part, links.bits[b])
        bit = (shard >> b) % 2
        part = jnp.where(
            bit == 0, jnp.concatenate([part, got], 0), jnp.concatenate([got, part], 0)
        )
    return part


def sum_small(links, vector):
    for pairs in [links.core, links.x] + links.bits:
        vector = vector + links.send(vector, pairs)
    return vector


def on_device(
    links,
    tokens,
    cotangent,
    lengths,
    joint_weight,
    query_bias,
    value_bias,
    output_weight,
    output_bias,
    norm_gain,
    norm_shift,
    expand_weight,
    expand_bias,
    reduce_weight,
    reduce_bias,
    final_gain,
    final_shift,
):
    owned = (
        joint_weight,
        query_bias,
        value_bias,
        output_weight,
        output_bias,
        norm_gain,
        norm_shift,
        expand_weight,
        expand_bias,
        reduce_weight,
        reduce_bias,
        final_gain,
        final_shift,
    )
    small = gather_small(links, jnp.concatenate([param for param in owned if param.ndim == 1]))
    marks = None
    full = []
    start = 0
    for param in owned:
        if param.ndim == 1:
            full.append(small[:, start : start + param.shape[0]].reshape(-1))
            start += param.shape[0]
        else:
            whole, marks = gather_weight(links, param, marks)
            full.append(whole)
    full_params = tuple(full)
    row_count, model_width = tokens.shape
    segment = segment_of(lengths[0], row_count)
    live_rows = (segment < lengths.shape[1]).astype(jnp.float32)[:, None]
    joint = jnp.dot(tokens, full_params[0], preferred_element_type=jnp.float32)
    queries = (joint[:, :model_width] + full_params[1].astype(jnp.float32)).astype(jnp.bfloat16)
    key_rows = joint[:, model_width : 2 * model_width].astype(jnp.bfloat16)
    values = (joint[:, 2 * model_width :] + full_params[2].astype(jnp.float32)).astype(jnp.bfloat16)
    context, log_total = attend_forward(queries, key_rows, values, segment, HEADS)
    branch = jnp.dot(context, full_params[3], preferred_element_type=jnp.float32) + full_params[
        4
    ].astype(jnp.float32)
    middle, middle_pull = jax.vjp(
        layer_norm,
        tokens.astype(jnp.float32) + branch,
        full_params[5].astype(jnp.float32),
        full_params[6].astype(jnp.float32),
    )
    middle_low = middle.astype(jnp.bfloat16)
    hidden = jnp.dot(middle_low, full_params[7], preferred_element_type=jnp.float32) + full_params[
        8
    ].astype(jnp.float32)
    active_full, gelu_pull = jax.vjp(gelu_exact, hidden)
    active = active_full.astype(jnp.bfloat16)
    second = jnp.dot(active, full_params[9], preferred_element_type=jnp.float32) + full_params[
        10
    ].astype(jnp.float32)

    def final_norm(inputs, gain_vector, shift_vector):
        return layer_norm(inputs, gain_vector, shift_vector) * live_rows

    output, final_pull = jax.vjp(
        final_norm,
        middle + second,
        full_params[11].astype(jnp.float32),
        full_params[12].astype(jnp.float32),
    )
    back_params = full_params
    grad_two, grad_final_gain, grad_final_shift = final_pull(cotangent.astype(jnp.float32))
    grad_second = grad_two.astype(jnp.bfloat16)
    grad_reduce_weight = jnp.einsum(
        "tf,td->fd", active, grad_second, preferred_element_type=jnp.float32
    ).astype(jnp.bfloat16)
    grad_reduce_bias = jnp.sum(grad_second.astype(jnp.float32), axis=0)
    sum_reduce, marks = reduce_weight_grad(links, grad_reduce_weight, None)
    grad_active = jnp.einsum(
        "td,fd->tf", after(grad_second, grad_reduce_weight), back_params[9], preferred_element_type=jnp.float32
    )
    grad_hidden = gelu_pull(grad_active)[0].astype(jnp.bfloat16)
    grad_expand_weight = jnp.einsum(
        "td,tf->df", middle_low, grad_hidden, preferred_element_type=jnp.float32
    ).astype(jnp.bfloat16)
    grad_expand_bias = jnp.sum(grad_hidden.astype(jnp.float32), axis=0)
    sum_expand, marks = reduce_weight_grad(links, grad_expand_weight, marks)
    grad_middle = grad_two + jnp.einsum(
        "tf,df->td", after(grad_hidden, grad_expand_weight), back_params[7], preferred_element_type=jnp.float32
    )
    ffn_grads = (
        grad_expand_weight,
        grad_expand_bias,
        grad_reduce_weight,
        grad_reduce_bias,
        grad_final_gain,
        grad_final_shift,
    )
    grad_one, grad_norm_gain, grad_norm_shift = middle_pull(grad_middle)
    grad_branch = grad_one.astype(jnp.bfloat16)
    grad_output_weight = jnp.einsum(
        "td,te->de", context, grad_branch, preferred_element_type=jnp.float32
    ).astype(jnp.bfloat16)
    grad_output_bias = jnp.sum(grad_branch.astype(jnp.float32), axis=0)
    sum_output, marks = reduce_weight_grad(links, grad_output_weight, marks)
    grad_context = jnp.einsum(
        "te,de->td", after(grad_branch, grad_output_weight), back_params[3], preferred_element_type=jnp.float32
    ).astype(jnp.bfloat16)
    grad_queries, grad_keys, grad_values = attend_backward(
        queries, key_rows, values, segment, log_total, grad_context, HEADS
    )
    grad_joint = jnp.concatenate(
        [
            grad_queries.astype(jnp.bfloat16),
            grad_keys.astype(jnp.bfloat16),
            grad_values.astype(jnp.bfloat16),
        ],
        axis=1,
    )
    grad_query_bias = jnp.sum(grad_joint[:, :model_width].astype(jnp.float32), axis=0)
    grad_value_bias = jnp.sum(grad_joint[:, 2 * model_width :].astype(jnp.float32), axis=0)
    grad_joint_weight = jnp.einsum(
        "td,te->de", tokens, grad_joint, preferred_element_type=jnp.float32
    ).astype(jnp.bfloat16)
    sum_joint, marks = reduce_weight_grad(links, grad_joint_weight, marks)
    grad_tokens = (
        grad_one
        + jnp.einsum("te,de->td", after(grad_joint, grad_joint_weight), back_params[0], preferred_element_type=jnp.float32)
    ).astype(jnp.bfloat16)
    attn_grads = (
        grad_joint_weight,
        grad_query_bias,
        grad_value_bias,
        grad_output_weight,
        grad_output_bias,
        grad_norm_gain,
        grad_norm_shift,
    )
    every = attn_grads + ffn_grads
    vectors = [grad for grad in every if grad.ndim == 1]
    summed = sum_small(links, jnp.concatenate(vectors))
    shard = lax.axis_index("shard")
    small_sums = []
    start = 0
    for vector in vectors:
        size = vector.shape[0] // links.shard_count
        small_sums.append(lax.dynamic_slice(summed, (start + shard * size,), (size,)))
        start += vector.shape[0]
    small_sums = iter(small_sums)
    large_sums = iter([sum_joint, sum_output, sum_expand, sum_reduce])
    every_grad = [next(small_sums) if grad.ndim == 1 else next(large_sums) for grad in every]
    attn_grads = every_grad[:7]
    ffn_grads = every_grad[7:]
    return (
        output.astype(jnp.bfloat16),
        grad_tokens,
        attn_grads[0],
        attn_grads[1],
        attn_grads[2],
        attn_grads[3],
        attn_grads[4],
        attn_grads[5],
        attn_grads[6],
        ffn_grads[0],
        ffn_grads[1],
        ffn_grads[2],
        ffn_grads[3],
        ffn_grads[4],
        ffn_grads[5],
    )


def solution(mesh):
    placed = (
        P(("rep", "shard"), None),
        P(("rep", "shard"), None),
        P(("rep", "shard"), None),
        P("shard", None),
        P("shard"),
        P("shard"),
        P("shard", None),
        P("shard"),
        P("shard"),
        P("shard"),
        P("shard", None),
        P("shard"),
        P("shard", None),
        P("shard"),
        P("shard"),
        P("shard"),
    )
    return jax.shard_map(
        functools.partial(on_device, Links(mesh)),
        mesh=mesh,
        in_specs=placed,
        out_specs=(
            P(("rep", "shard"), None),
            P(("rep", "shard"), None),
            P("shard", None),
            P("shard"),
            P("shard"),
            P("shard", None),
            P("shard"),
            P("shard"),
            P("shard"),
            P("shard", None),
            P("shard"),
            P("shard", None),
            P("shard"),
            P("shard"),
            P("shard"),
        ),
        check_vma=False,
    )
```

```python
import functools

import jax
import jax.numpy as jnp
from jax import lax
from jax.sharding import PartitionSpec as P

HEADS = 16


epsilon = 1e-05
mask_fill = -1000000000.0


def layer_norm(inputs, gain_vector, shift_vector):
    centre = inputs - jnp.mean(inputs, axis=-1, keepdims=True)
    variance = jnp.mean(centre * centre, axis=-1, keepdims=True)
    return centre * lax.rsqrt(variance + epsilon) * gain_vector + shift_vector


def gelu_exact(inputs):
    return 0.5 * inputs * (1.0 + jax.scipy.special.erf(inputs * 0.7071067811865476))


def segment_of(length_row, row_count):
    seq_ends = jnp.cumsum(length_row)
    position = jnp.arange(row_count, dtype=jnp.int32)
    return jnp.sum((position[:, None] >= seq_ends[None, :]).astype(jnp.int32), axis=1)


def block_scores(query_block, key_heads, segment_block, segment, score_scale):
    scores = (
        jnp.einsum("qhd,khd->hqk", query_block, key_heads, preferred_element_type=jnp.float32)
        * score_scale
    )
    return jnp.where((segment_block[:, None] == segment[None, :])[None], scores, mask_fill)


def attend_forward(queries, key_rows, values, segment, head_count):
    row_count, model_width = queries.shape
    head_size = model_width // head_count
    block_size = min(512, row_count)
    score_scale = head_size ** (-0.5)
    key_heads = key_rows.reshape(row_count, head_count, head_size)
    value_heads = values.reshape(row_count, head_count, head_size)

    def one_block(state_carry, block_index):
        query_block = queries.reshape(block_size, head_count, head_size)
        scores = block_scores(query_block, key_heads, segment, segment, score_scale)
        row_max = jnp.max(scores, axis=-1, keepdims=True)
        powers = jnp.exp(scores - row_max)
        row_total = jnp.sum(powers, axis=-1, keepdims=True)
        attn_weights = (powers / row_total).astype(jnp.bfloat16)
        context = jnp.einsum(
            "hqk,khd->qhd", attn_weights, value_heads, preferred_element_type=jnp.float32
        )
        log_total = (row_max + jnp.log(row_total))[..., 0]
        return (
            state_carry,
            (context.reshape(block_size, model_width).astype(jnp.bfloat16), log_total),
        )

    _, (context, log_total) = lax.scan(one_block, 0, jnp.arange(row_count // block_size))
    return (context.reshape(row_count, model_width), log_total)


def attend_backward(queries, key_rows, values, segment, log_total, grad_context, head_count):
    row_count, model_width = queries.shape
    head_size = model_width // head_count
    block_size = min(512, row_count)
    score_scale = head_size ** (-0.5)
    key_heads = key_rows.reshape(row_count, head_count, head_size)
    value_heads = values.reshape(row_count, head_count, head_size)

    def one_block(state_carry, block_items):
        grad_keys, grad_values = state_carry
        block_index, block_total = block_items
        query_block = queries.reshape(block_size, head_count, head_size)
        grad_block = grad_context.reshape(block_size, head_count, head_size)
        scores = block_scores(query_block, key_heads, segment, segment, score_scale)
        attn_weights = jnp.exp(scores - block_total[..., None])
        grad_weights = jnp.einsum(
            "qhd,khd->hqk", grad_block, value_heads, preferred_element_type=jnp.float32
        )
        inner = jnp.sum(attn_weights * grad_weights, axis=-1, keepdims=True)
        grad_scores = (attn_weights * (grad_weights - inner)).astype(jnp.bfloat16)
        grad_query = (
            jnp.einsum("hqk,khd->qhd", grad_scores, key_heads, preferred_element_type=jnp.float32)
            * score_scale
        )
        grad_keys = (
            grad_keys
            + jnp.einsum(
                "hqk,qhd->khd", grad_scores, query_block, preferred_element_type=jnp.float32
            )
            * score_scale
        )
        grad_values = grad_values + jnp.einsum(
            "hqk,qhd->khd",
            attn_weights.astype(jnp.bfloat16),
            grad_block,
            preferred_element_type=jnp.float32,
        )
        return ((grad_keys, grad_values), grad_query.reshape(block_size, model_width))

    zero_heads = jnp.zeros((row_count, head_count, head_size), jnp.float32)
    (grad_keys, grad_values), grad_queries = lax.scan(
        one_block, (zero_heads, zero_heads), (jnp.arange(row_count // block_size), log_total)
    )
    return (
        grad_queries.reshape(row_count, model_width),
        grad_keys.reshape(row_count, model_width),
        grad_values.reshape(row_count, model_width),
    )


def flip_pairs(rep_count, shard_count, rep_bit, shard_bit):
    pairs = []
    for rep in range(rep_count):
        for shard in range(shard_count):
            to_rep = rep ^ rep_bit[rep % 2]
            to_shard = shard ^ shard_bit[rep % 2]
            pairs.append((rep * shard_count + shard, to_rep * shard_count + to_shard))
    return pairs


class Links:
    def __init__(self, mesh):
        rep_count, shard_count = mesh.shape["rep"], mesh.shape["shard"]
        self.rep_count, self.shard_count = rep_count, shard_count
        self.shard_bits = shard_count.bit_length() - 1

        def pairs(rep_bit, shard_bit):
            return flip_pairs(rep_count, shard_count, rep_bit, shard_bit)

        self.core = pairs((1, 1), (0, 0))
        self.x = pairs((2, 2), (0, 0))
        self.first = pairs((2, 0), (0, 1))
        self.second = pairs((0, 2), (1, 0))
        self.bits = [pairs((0, 0), (1 << b, 1 << b)) for b in range(self.shard_bits)]

    def send(self, array, pairs):
        return lax.ppermute(array, ("rep", "shard"), pairs)


def after(array, marker):
    if marker is None:
        return array
    return lax.optimization_barrier((array, marker))[0]


def take(array, index, axis):
    return lax.dynamic_index_in_dim(array, index, axis, keepdims=False)


def put_pair(mine, other, bit, axis):
    return jnp.where(bit == 0, jnp.stack([mine, other], axis), jnp.stack([other, mine], axis))


def place():
    rep, shard = lax.axis_index("rep"), lax.axis_index("shard")
    return rep % 2, rep // 2, shard


def add_low(mine, got):
    return (mine.astype(jnp.float32) + got.astype(jnp.float32)).astype(jnp.bfloat16)


def gather_chunk(links, owns):
    core, x, shard = place()
    rows = owns[0].shape[0]
    quarter = rows // 4
    widths = [own.shape[1] for own in owns]
    width = sum(widths)

    def quarter_of(own):
        return take(take(own.reshape(2, 2, quarter, own.shape[1]), x, 0), core, 0)

    part = jnp.concatenate([quarter_of(own) for own in owns], axis=1)[None]
    for b in range(links.shard_bits - 1, 0, -1):
        got = yield (part, links.bits[b])
        part = put_pair(part, got, (shard >> b) % 2, 1).reshape(-1, quarter, width)
    lead = part.shape[0]
    mine_q = (shard % 2) * 2 + x
    got = yield (part, links.second)
    pair = jnp.stack([part, got], axis=1)
    got = yield (pair, links.first)
    four = jnp.concatenate([pair, got], axis=1)
    blocks = []
    for q in range(4):
        apart = q ^ mine_q
        swapped = (apart % 2) * 2 + apart // 2
        blocks.append(take(four, jnp.where(core == 0, swapped, apart), 1))
    near = jnp.stack(blocks, axis=1)
    far = yield (near, links.core)
    zero = jnp.int32(0)
    wholes = []
    start = 0
    for size in widths:
        whole = jnp.zeros((lead, 4, 2, quarter, size), part.dtype)
        for block, side in ((near, core), (far, 1 - core)):
            block = block[:, :, None, :, start : start + size]
            whole = lax.dynamic_update_slice(whole, block, (zero, zero, side, zero, zero))
        wholes.append(whole.reshape(rows * links.shard_count, size))
        start += size
    return wholes


def reduce_chunk(links, grads):
    core, x, shard = place()
    rows = grads[0].shape[0] // links.shard_count
    quarter = rows // 4
    lead = links.shard_count // 2
    widths = [grad.shape[1] for grad in grads]
    width = sum(widths)

    def side_of(side):
        views = [grad.reshape(lead, 4, 2, quarter, grad.shape[1]) for grad in grads]
        return jnp.concatenate([take(view, side, 2) for view in views], axis=-1)

    got = yield (side_of(1 - core), links.core)
    four = add_low(side_of(core), got)
    final_q = (shard % 2) * 2 + x
    mid_q = jnp.where(core == 0, final_q ^ 2, final_q ^ 1)
    away_final = jnp.where(core == 0, final_q ^ 1, final_q ^ 2)
    away = jnp.stack([take(four, away_final, 1), take(four, 3 - final_q, 1)], axis=1)
    got = yield (away, links.first)
    mid = add_low(take(four, mid_q, 1), got[:, 1])
    final = take(four, final_q, 1).astype(jnp.float32) + got[:, 0].astype(jnp.float32)
    got = yield (mid, links.second)
    total = (final + got.astype(jnp.float32)).astype(jnp.bfloat16)
    for b in range(1, links.shard_bits):
        bit = (shard >> b) % 2
        pairs = total.reshape(-1, 2, quarter, width)
        got = yield (take(pairs, 1 - bit, 1), links.bits[b])
        total = add_low(take(pairs, bit, 1), got)
    total = total.reshape(quarter, width)
    got = yield (total, links.x)
    both_x = put_pair(total, got, x, 0)
    got = yield (both_x, links.core)
    both = put_pair(both_x, got, core, 1).reshape(rows, width).astype(jnp.float32)
    sums = []
    start = 0
    for size in widths:
        sums.append(both[:, start : start + size])
        start += size
    return sums


def gather_small(links, own):
    _, _, shard = place()
    part = own[None]
    for b in range(links.shard_bits):
        got = yield (part, links.bits[b])
        bit = (shard >> b) % 2
        part = jnp.where(
            bit == 0, jnp.concatenate([part, got], 0), jnp.concatenate([got, part], 0)
        )
    return part


def sum_small(links, vector):
    for pairs in [links.core, links.x] + links.bits:
        got = yield (vector, pairs)
        vector = vector + got
    return vector


class Ticks:
    def __init__(self, links):
        self.links = links
        self.waiting = {}
        self.done = {}

    def begin(self, name, stages):
        self.waiting[name] = (stages, next(stages))

    def tick(self, compute=None, inputs=()):
        names = list(self.waiting)
        operands = [self.waiting[name][1][0] for name in names]
        operands, inputs = lax.optimization_barrier((operands, tuple(inputs)))
        gots = [
            self.links.send(operand, self.waiting[name][1][1])
            for operand, name in zip(operands, names)
        ]
        outs = compute(*inputs) if compute is not None else ()
        gots, outs = lax.optimization_barrier((gots, outs))
        for name, got in zip(names, gots):
            stages = self.waiting[name][0]
            try:
                self.waiting[name] = (stages, stages.send(got))
            except StopIteration as finished:
                self.done[name] = finished.value
                del self.waiting[name]
        return outs

    def finish(self, *names):
        while any(name not in self.done for name in names):
            self.tick()
        return [self.done[name] for name in names]


def on_device(
    links,
    tokens,
    cotangent,
    lengths,
    joint_weight,
    query_bias,
    value_bias,
    output_weight,
    output_bias,
    norm_gain,
    norm_shift,
    expand_weight,
    expand_bias,
    reduce_weight,
    reduce_bias,
    final_gain,
    final_shift,
):
    owned = (
        joint_weight,
        query_bias,
        value_bias,
        output_weight,
        output_bias,
        norm_gain,
        norm_shift,
        expand_weight,
        expand_bias,
        reduce_weight,
        reduce_bias,
        final_gain,
        final_shift,
    )
    ticks = Ticks(links)
    ticks.begin("joint", gather_chunk(links, [joint_weight]))
    ticks.begin("small", gather_small(links, jnp.concatenate([p for p in owned if p.ndim == 1])))
    ticks.tick()
    ticks.begin("wide", gather_chunk(links, [expand_weight, output_weight]))
    ticks.tick()
    ticks.begin("reduce", gather_chunk(links, [reduce_weight]))
    (joint_full,), small = ticks.finish("joint", "small")
    vectors = []
    start = 0
    for param in owned:
        if param.ndim == 1:
            whole = small[:, start : start + param.shape[0]].reshape(-1)
            vectors.append(whole.astype(jnp.float32))
            start += param.shape[0]
    query_add, value_add, output_add, gain_one, shift_one, expand_add, reduce_add, gain_two, shift_two = (
        vectors
    )

    row_count, model_width = tokens.shape
    segment = segment_of(lengths[0], row_count)
    live_rows = (segment < lengths.shape[1]).astype(jnp.float32)[:, None]

    def attend(tokens, weight):
        joint = jnp.dot(tokens, weight, preferred_element_type=jnp.float32)
        queries = (joint[:, :model_width] + query_add).astype(jnp.bfloat16)
        key_rows = joint[:, model_width : 2 * model_width].astype(jnp.bfloat16)
        values = (joint[:, 2 * model_width :] + value_add).astype(jnp.bfloat16)
        context, log_total = attend_forward(queries, key_rows, values, segment, HEADS)
        return queries, key_rows, values, context, log_total

    queries, key_rows, values, context, log_total = ticks.tick(attend, (tokens, joint_full))
    ((expand_full, output_full),) = ticks.finish("wide")

    def to_active(context, expand_full, output_full):
        branch = jnp.dot(context, output_full, preferred_element_type=jnp.float32) + output_add
        normed = tokens.astype(jnp.float32) + branch
        middle = layer_norm(normed, gain_one, shift_one)
        middle_low = middle.astype(jnp.bfloat16)
        hidden = jnp.dot(middle_low, expand_full, preferred_element_type=jnp.float32) + expand_add
        return normed, middle, middle_low, hidden, gelu_exact(hidden).astype(jnp.bfloat16)

    normed, middle, middle_low, hidden, active = ticks.tick(
        to_active, (context, expand_full, output_full)
    )
    ((reduce_full,),) = ticks.finish("reduce")
    second = jnp.dot(active, reduce_full, preferred_element_type=jnp.float32) + reduce_add

    def final_norm(inputs, gain_vector, shift_vector):
        return layer_norm(inputs, gain_vector, shift_vector) * live_rows

    output, final_pull = jax.vjp(final_norm, middle + second, gain_two, shift_two)
    grad_two, grad_final_gain, grad_final_shift = final_pull(cotangent.astype(jnp.float32))
    grad_second = grad_two.astype(jnp.bfloat16)
    grad_reduce_weight = jnp.einsum(
        "tf,td->fd", active, grad_second, preferred_element_type=jnp.float32
    ).astype(jnp.bfloat16)
    grad_reduce_bias = jnp.sum(grad_second.astype(jnp.float32), axis=0)
    ticks.begin("grad_reduce", reduce_chunk(links, [grad_reduce_weight]))

    def hidden_back(grad_second, hidden, middle_low):
        grad_active = jnp.einsum(
            "td,fd->tf", grad_second, reduce_full, preferred_element_type=jnp.float32
        )
        _, gelu_pull = jax.vjp(gelu_exact, hidden)
        grad_hidden = gelu_pull(grad_active)[0].astype(jnp.bfloat16)
        grad_expand_weight = jnp.einsum(
            "td,tf->df", middle_low, grad_hidden, preferred_element_type=jnp.float32
        ).astype(jnp.bfloat16)
        return grad_hidden, grad_expand_weight

    grad_hidden, grad_expand_weight = ticks.tick(hidden_back, (grad_second, hidden, middle_low))
    grad_expand_bias = jnp.sum(grad_hidden.astype(jnp.float32), axis=0)

    def middle_back(grad_hidden, grad_two, normed, context):
        grad_middle = grad_two + jnp.einsum(
            "tf,df->td", grad_hidden, expand_full, preferred_element_type=jnp.float32
        )
        _, middle_pull = jax.vjp(layer_norm, normed, gain_one, shift_one)
        grad_one, grad_norm_gain, grad_norm_shift = middle_pull(grad_middle)
        grad_branch = grad_one.astype(jnp.bfloat16)
        grad_output_weight = jnp.einsum(
            "td,te->de", context, grad_branch, preferred_element_type=jnp.float32
        ).astype(jnp.bfloat16)
        return grad_one, grad_norm_gain, grad_norm_shift, grad_branch, grad_output_weight

    grad_one, grad_norm_gain, grad_norm_shift, grad_branch, grad_output_weight = ticks.tick(
        middle_back, (grad_hidden, grad_two, normed, context)
    )
    ticks.begin("grad_wide", reduce_chunk(links, [grad_expand_weight, grad_output_weight]))
    grad_output_bias = jnp.sum(grad_branch.astype(jnp.float32), axis=0)
    grad_context = jnp.einsum(
        "te,de->td", grad_branch, output_full, preferred_element_type=jnp.float32
    ).astype(jnp.bfloat16)
    parts = []
    groups = 2
    group_width = model_width // groups
    group_heads = HEADS // groups
    for group in range(groups):
        columns = slice(group * group_width, (group + 1) * group_width)

        def heads_back(queries, key_rows, values, grad_context, log_total):
            grads = attend_backward(
                queries, key_rows, values, segment, log_total, grad_context, group_heads
            )
            return tuple(grad.astype(jnp.bfloat16) for grad in grads)

        if parts:
            grad_context = after(grad_context, parts[-1])
        parts.append(
            ticks.tick(
                heads_back,
                (
                    queries[:, columns],
                    key_rows[:, columns],
                    values[:, columns],
                    grad_context[:, columns],
                    log_total[:, group * group_heads : (group + 1) * group_heads],
                ),
            )
        )
    grad_joint = jnp.concatenate(
        [parts[group][which] for which in range(3) for group in range(groups)], axis=1
    )
    grad_query_bias = jnp.sum(grad_joint[:, :model_width].astype(jnp.float32), axis=0)
    grad_value_bias = jnp.sum(grad_joint[:, 2 * model_width :].astype(jnp.float32), axis=0)

    def joint_back(tokens, grad_joint):
        return jnp.einsum(
            "td,te->de", tokens, grad_joint, preferred_element_type=jnp.float32
        ).astype(jnp.bfloat16)

    grad_joint_weight = ticks.tick(joint_back, (tokens, grad_joint))
    ticks.begin("grad_joint", reduce_chunk(links, [grad_joint_weight]))
    vectors = [
        grad_query_bias,
        grad_value_bias,
        grad_output_bias,
        grad_norm_gain,
        grad_norm_shift,
        grad_expand_bias,
        grad_reduce_bias,
        grad_final_gain,
        grad_final_shift,
    ]
    ticks.begin("grad_small", sum_small(links, jnp.concatenate(vectors)))

    def tokens_back(grad_one, grad_joint):
        return (
            grad_one
            + jnp.einsum("te,de->td", grad_joint, joint_full, preferred_element_type=jnp.float32)
        ).astype(jnp.bfloat16)

    grad_tokens = ticks.tick(tokens_back, (grad_one, grad_joint))
    (sum_joint,), (sum_expand, sum_output), (sum_reduce,), summed = ticks.finish(
        "grad_joint", "grad_wide", "grad_reduce", "grad_small"
    )
    shard = lax.axis_index("shard")
    small_sums = []
    start = 0
    for vector in vectors:
        size = vector.shape[0] // links.shard_count
        small_sums.append(lax.dynamic_slice(summed, (start + shard * size,), (size,)))
        start += vector.shape[0]
    attn_grads = (sum_joint, *small_sums[:2], sum_output, *small_sums[2:5])
    ffn_grads = (sum_expand, small_sums[5], sum_reduce, *small_sums[6:])
    return (
        output.astype(jnp.bfloat16),
        grad_tokens,
        attn_grads[0],
        attn_grads[1],
        attn_grads[2],
        attn_grads[3],
        attn_grads[4],
        attn_grads[5],
        attn_grads[6],
        ffn_grads[0],
        ffn_grads[1],
        ffn_grads[2],
        ffn_grads[3],
        ffn_grads[4],
        ffn_grads[5],
    )


def solution(mesh):
    placed = (
        P(("rep", "shard"), None),
        P(("rep", "shard"), None),
        P(("rep", "shard"), None),
        P("shard", None),
        P("shard"),
        P("shard"),
        P("shard", None),
        P("shard"),
        P("shard"),
        P("shard"),
        P("shard", None),
        P("shard"),
        P("shard", None),
        P("shard"),
        P("shard"),
        P("shard"),
    )
    return jax.shard_map(
        functools.partial(on_device, Links(mesh)),
        mesh=mesh,
        in_specs=placed,
        out_specs=(
            P(("rep", "shard"), None),
            P(("rep", "shard"), None),
            P("shard", None),
            P("shard"),
            P("shard"),
            P("shard", None),
            P("shard"),
            P("shard"),
            P("shard"),
            P("shard", None),
            P("shard"),
            P("shard", None),
            P("shard"),
            P("shard"),
            P("shard"),
        ),
        check_vma=False,
    )
```

```python
import functools

import jax
import jax.numpy as jnp
from jax import lax
from jax.sharding import PartitionSpec as P

HEADS = 16


epsilon = 1e-05
mask_fill = -1000000000.0


def layer_norm(inputs, gain_vector, shift_vector):
    centre = inputs - jnp.mean(inputs, axis=-1, keepdims=True)
    variance = jnp.mean(centre * centre, axis=-1, keepdims=True)
    return centre * lax.rsqrt(variance + epsilon) * gain_vector + shift_vector


def gelu_exact(inputs):
    return 0.5 * inputs * (1.0 + jax.scipy.special.erf(inputs * 0.7071067811865476))


def segment_of(length_row, row_count):
    seq_ends = jnp.cumsum(length_row)
    position = jnp.arange(row_count, dtype=jnp.int32)
    return jnp.sum((position[:, None] >= seq_ends[None, :]).astype(jnp.int32), axis=1)


def block_scores(query_block, key_heads, segment_block, segment, score_scale):
    scores = (
        jnp.einsum("qhd,khd->hqk", query_block, key_heads, preferred_element_type=jnp.float32)
        * score_scale
    )
    return jnp.where((segment_block[:, None] == segment[None, :])[None], scores, mask_fill)


def attend_forward(queries, key_rows, values, segment, head_count):
    row_count, model_width = queries.shape
    head_size = model_width // head_count
    block_size = min(512, row_count)
    score_scale = head_size ** (-0.5)
    key_heads = key_rows.reshape(row_count, head_count, head_size)
    value_heads = values.reshape(row_count, head_count, head_size)

    def one_block(state_carry, block_index):
        query_block = queries.reshape(block_size, head_count, head_size)
        scores = block_scores(query_block, key_heads, segment, segment, score_scale)
        row_max = jnp.max(scores, axis=-1, keepdims=True)
        powers = jnp.exp(scores - row_max)
        row_total = jnp.sum(powers, axis=-1, keepdims=True)
        attn_weights = (powers / row_total).astype(jnp.bfloat16)
        context = jnp.einsum(
            "hqk,khd->qhd", attn_weights, value_heads, preferred_element_type=jnp.float32
        )
        log_total = (row_max + jnp.log(row_total))[..., 0]
        return (
            state_carry,
            (context.reshape(block_size, model_width).astype(jnp.bfloat16), log_total),
        )

    _, (context, log_total) = lax.scan(one_block, 0, jnp.arange(row_count // block_size))
    return (context.reshape(row_count, model_width), log_total)


def attend_backward(queries, key_rows, values, segment, log_total, grad_context, head_count):
    row_count, model_width = queries.shape
    head_size = model_width // head_count
    block_size = min(512, row_count)
    score_scale = head_size ** (-0.5)
    key_heads = key_rows.reshape(row_count, head_count, head_size)
    value_heads = values.reshape(row_count, head_count, head_size)

    def one_block(state_carry, block_items):
        grad_keys, grad_values = state_carry
        block_index, block_total = block_items
        query_block = queries.reshape(block_size, head_count, head_size)
        grad_block = grad_context.reshape(block_size, head_count, head_size)
        scores = block_scores(query_block, key_heads, segment, segment, score_scale)
        attn_weights = jnp.exp(scores - block_total[..., None])
        grad_weights = jnp.einsum(
            "qhd,khd->hqk", grad_block, value_heads, preferred_element_type=jnp.float32
        )
        inner = jnp.sum(attn_weights * grad_weights, axis=-1, keepdims=True)
        grad_scores = (attn_weights * (grad_weights - inner)).astype(jnp.bfloat16)
        grad_query = (
            jnp.einsum("hqk,khd->qhd", grad_scores, key_heads, preferred_element_type=jnp.float32)
            * score_scale
        )
        grad_keys = (
            grad_keys
            + jnp.einsum(
                "hqk,qhd->khd", grad_scores, query_block, preferred_element_type=jnp.float32
            )
            * score_scale
        )
        grad_values = grad_values + jnp.einsum(
            "hqk,qhd->khd",
            attn_weights.astype(jnp.bfloat16),
            grad_block,
            preferred_element_type=jnp.float32,
        )
        return ((grad_keys, grad_values), grad_query.reshape(block_size, model_width))

    zero_heads = jnp.zeros((row_count, head_count, head_size), jnp.float32)
    (grad_keys, grad_values), grad_queries = lax.scan(
        one_block, (zero_heads, zero_heads), (jnp.arange(row_count // block_size), log_total)
    )
    return (
        grad_queries.reshape(row_count, model_width),
        grad_keys.reshape(row_count, model_width),
        grad_values.reshape(row_count, model_width),
    )


def flip_pairs(rep_count, shard_count, rep_bit, shard_bit):
    pairs = []
    for rep in range(rep_count):
        for shard in range(shard_count):
            to_rep = rep ^ rep_bit[rep % 2]
            to_shard = shard ^ shard_bit[rep % 2]
            pairs.append((rep * shard_count + shard, to_rep * shard_count + to_shard))
    return pairs


class Links:
    def __init__(self, mesh):
        rep_count, shard_count = mesh.shape["rep"], mesh.shape["shard"]
        self.rep_count, self.shard_count = rep_count, shard_count
        self.shard_bits = shard_count.bit_length() - 1

        def pairs(rep_bit, shard_bit):
            return flip_pairs(rep_count, shard_count, rep_bit, shard_bit)

        self.core = pairs((1, 1), (0, 0))
        self.x = pairs((2, 2), (0, 0))
        self.first = pairs((2, 0), (0, 1))
        self.second = pairs((0, 2), (1, 0))
        self.bits = [pairs((0, 0), (1 << b, 1 << b)) for b in range(self.shard_bits)]

    def send(self, array, pairs):
        return lax.ppermute(array, ("rep", "shard"), pairs)


def after(array, marker):
    if marker is None:
        return array
    return lax.optimization_barrier((array, marker))[0]


def take(array, index, axis):
    return lax.dynamic_index_in_dim(array, index, axis, keepdims=False)


def put_pair(mine, other, bit, axis):
    return jnp.where(bit == 0, jnp.stack([mine, other], axis), jnp.stack([other, mine], axis))


def place():
    rep, shard = lax.axis_index("rep"), lax.axis_index("shard")
    return rep % 2, rep // 2, shard


def add_low(mine, got):
    return (mine.astype(jnp.float32) + got.astype(jnp.float32)).astype(jnp.bfloat16)


def gather_chunk(links, owns):
    core, x, shard = place()
    rows = owns[0].shape[0]
    quarter = rows // 4
    widths = [own.shape[1] for own in owns]
    width = sum(widths)

    def quarter_of(own):
        return take(take(own.reshape(2, 2, quarter, own.shape[1]), x, 0), core, 0)

    part = jnp.concatenate([quarter_of(own) for own in owns], axis=1)[None]
    for b in range(links.shard_bits - 1, 0, -1):
        got = yield (part, links.bits[b])
        part = put_pair(part, got, (shard >> b) % 2, 1).reshape(-1, quarter, width)
    lead = part.shape[0]
    mine_q = (shard % 2) * 2 + x
    got = yield (part, links.second)
    pair = jnp.stack([part, got], axis=1)
    got = yield (pair, links.first)
    four = jnp.concatenate([pair, got], axis=1)
    blocks = []
    for q in range(4):
        apart = q ^ mine_q
        swapped = (apart % 2) * 2 + apart // 2
        blocks.append(take(four, jnp.where(core == 0, swapped, apart), 1))
    near = jnp.stack(blocks, axis=1)
    far = yield (near, links.core)
    wholes = []
    start = 0
    for size in widths:
        columns = slice(start, start + size)
        first = jnp.where(core == 0, near[..., columns], far[..., columns])
        second = jnp.where(core == 0, far[..., columns], near[..., columns])
        whole = jnp.stack([first, second], axis=2)
        wholes.append(whole.reshape(rows * links.shard_count, size))
        start += size
    return wholes


def reduce_chunk(links, grads):
    core, x, shard = place()
    rows = grads[0].shape[0] // links.shard_count
    quarter = rows // 4
    lead = links.shard_count // 2
    widths = [grad.shape[1] for grad in grads]
    width = sum(widths)

    def side_of(side):
        views = [grad.reshape(lead, 4, 2, quarter, grad.shape[1]) for grad in grads]
        return jnp.concatenate([take(view, side, 2) for view in views], axis=-1)

    got = yield (side_of(1 - core), links.core)
    four = add_low(side_of(core), got)
    final_q = (shard % 2) * 2 + x
    mid_q = jnp.where(core == 0, final_q ^ 2, final_q ^ 1)
    away_final = jnp.where(core == 0, final_q ^ 1, final_q ^ 2)
    away = jnp.stack([take(four, away_final, 1), take(four, 3 - final_q, 1)], axis=1)
    got = yield (away, links.first)
    mid = add_low(take(four, mid_q, 1), got[:, 1])
    final = take(four, final_q, 1).astype(jnp.float32) + got[:, 0].astype(jnp.float32)
    got = yield (mid, links.second)
    total = (final + got.astype(jnp.float32)).astype(jnp.bfloat16)
    for b in range(1, links.shard_bits):
        bit = (shard >> b) % 2
        pairs = total.reshape(-1, 2, quarter, width)
        got = yield (take(pairs, 1 - bit, 1), links.bits[b])
        total = add_low(take(pairs, bit, 1), got)
    total = total.reshape(quarter, width)
    got = yield (total, links.x)
    both_x = put_pair(total, got, x, 0)
    got = yield (both_x, links.core)
    both = put_pair(both_x, got, core, 1).reshape(rows, width).astype(jnp.float32)
    sums = []
    start = 0
    for size in widths:
        sums.append(both[:, start : start + size])
        start += size
    return sums


def gather_small(links, own):
    _, _, shard = place()
    part = own[None]
    for b in range(links.shard_bits):
        got = yield (part, links.bits[b])
        bit = (shard >> b) % 2
        part = jnp.where(
            bit == 0, jnp.concatenate([part, got], 0), jnp.concatenate([got, part], 0)
        )
    return part


def sum_small(links, vector):
    for pairs in [links.core, links.x] + links.bits:
        got = yield (vector, pairs)
        vector = vector + got
    return vector


class Ticks:
    def __init__(self, links):
        self.links = links
        self.waiting = {}
        self.done = {}

    def begin(self, name, stages):
        self.waiting[name] = (stages, next(stages))

    def tick(self, compute=None, inputs=()):
        names = list(self.waiting)
        operands = [self.waiting[name][1][0] for name in names]
        operands, inputs = lax.optimization_barrier((operands, tuple(inputs)))
        gots = [
            self.links.send(operand, self.waiting[name][1][1])
            for operand, name in zip(operands, names)
        ]
        outs = compute(*inputs) if compute is not None else ()
        gots, outs = lax.optimization_barrier((gots, outs))
        for name, got in zip(names, gots):
            stages = self.waiting[name][0]
            try:
                self.waiting[name] = (stages, stages.send(got))
            except StopIteration as finished:
                self.done[name] = finished.value
                del self.waiting[name]
        return outs

    def finish(self, *names):
        while any(name not in self.done for name in names):
            self.tick()
        return [self.done[name] for name in names]


def on_device(
    links,
    tokens,
    cotangent,
    lengths,
    joint_weight,
    query_bias,
    value_bias,
    output_weight,
    output_bias,
    norm_gain,
    norm_shift,
    expand_weight,
    expand_bias,
    reduce_weight,
    reduce_bias,
    final_gain,
    final_shift,
):
    owned = (
        joint_weight,
        query_bias,
        value_bias,
        output_weight,
        output_bias,
        norm_gain,
        norm_shift,
        expand_weight,
        expand_bias,
        reduce_weight,
        reduce_bias,
        final_gain,
        final_shift,
    )
    ticks = Ticks(links)
    ticks.begin("joint", gather_chunk(links, [joint_weight]))
    ticks.begin("small", gather_small(links, jnp.concatenate([p for p in owned if p.ndim == 1])))
    ticks.tick()
    ticks.tick()
    ticks.begin("wide", gather_chunk(links, [expand_weight, output_weight]))
    ticks.tick()
    ticks.tick()
    ticks.begin("reduce", gather_chunk(links, [reduce_weight]))
    (joint_full,), small = ticks.finish("joint", "small")
    vectors = []
    start = 0
    for param in owned:
        if param.ndim == 1:
            whole = small[:, start : start + param.shape[0]].reshape(-1)
            vectors.append(whole.astype(jnp.float32))
            start += param.shape[0]
    query_add, value_add, output_add, gain_one, shift_one, expand_add, reduce_add, gain_two, shift_two = (
        vectors
    )

    row_count, model_width = tokens.shape
    segment = segment_of(lengths[0], row_count)
    live_rows = (segment < lengths.shape[1]).astype(jnp.float32)[:, None]

    groups = 2
    group_width = model_width // groups
    group_heads = HEADS // groups

    def columns_of(array, group):
        return array[:, group * group_width : (group + 1) * group_width]

    def attend_group(queries, key_rows, values, group):
        return attend_forward(
            columns_of(queries, group),
            columns_of(key_rows, group),
            columns_of(values, group),
            segment,
            group_heads,
        )

    def attend(tokens, weight):
        joint = jnp.dot(tokens, weight, preferred_element_type=jnp.float32)
        queries = (joint[:, :model_width] + query_add).astype(jnp.bfloat16)
        key_rows = joint[:, model_width : 2 * model_width].astype(jnp.bfloat16)
        values = (joint[:, 2 * model_width :] + value_add).astype(jnp.bfloat16)
        return queries, key_rows, values, attend_group(queries, key_rows, values, 0)

    queries, key_rows, values, attended = ticks.tick(attend, (tokens, joint_full))
    contexts, log_totals = [attended[0]], [attended[1]]
    for group in range(1, groups):
        more_context, more_log = ticks.tick(
            lambda *rows, group=group: attend_group(*rows, group), (queries, key_rows, values)
        )
        contexts.append(more_context)
        log_totals.append(more_log)
    context = jnp.concatenate(contexts, axis=1)
    ((expand_full, output_full),) = ticks.finish("wide")

    def to_active(context, expand_full, output_full):
        branch = jnp.dot(context, output_full, preferred_element_type=jnp.float32) + output_add
        normed = tokens.astype(jnp.float32) + branch
        middle = layer_norm(normed, gain_one, shift_one)
        middle_low = middle.astype(jnp.bfloat16)
        hidden = jnp.dot(middle_low, expand_full, preferred_element_type=jnp.float32) + expand_add
        return normed, middle, middle_low, hidden, gelu_exact(hidden).astype(jnp.bfloat16)

    normed, middle, middle_low, hidden, active = ticks.tick(
        to_active, (context, expand_full, output_full)
    )
    ((reduce_full,),) = ticks.finish("reduce")
    second = jnp.dot(active, reduce_full, preferred_element_type=jnp.float32) + reduce_add

    def final_norm(inputs, gain_vector, shift_vector):
        return layer_norm(inputs, gain_vector, shift_vector) * live_rows

    output, final_pull = jax.vjp(final_norm, middle + second, gain_two, shift_two)
    grad_two, grad_final_gain, grad_final_shift = final_pull(cotangent.astype(jnp.float32))
    grad_second = grad_two.astype(jnp.bfloat16)
    grad_reduce_weight = jnp.einsum(
        "tf,td->fd", active, grad_second, preferred_element_type=jnp.float32
    ).astype(jnp.bfloat16)
    grad_reduce_bias = jnp.sum(grad_second.astype(jnp.float32), axis=0)
    ticks.begin("grad_reduce", reduce_chunk(links, [grad_reduce_weight]))

    def hidden_back(grad_second, hidden, middle_low):
        grad_active = jnp.einsum(
            "td,fd->tf", grad_second, reduce_full, preferred_element_type=jnp.float32
        )
        _, gelu_pull = jax.vjp(gelu_exact, hidden)
        grad_hidden = gelu_pull(grad_active)[0].astype(jnp.bfloat16)
        grad_expand_weight = jnp.einsum(
            "td,tf->df", middle_low, grad_hidden, preferred_element_type=jnp.float32
        ).astype(jnp.bfloat16)
        return grad_hidden, grad_expand_weight

    grad_hidden, grad_expand_weight = ticks.tick(hidden_back, (grad_second, hidden, middle_low))
    grad_expand_bias = jnp.sum(grad_hidden.astype(jnp.float32), axis=0)

    def middle_back(grad_hidden, grad_two, normed, context):
        grad_middle = grad_two + jnp.einsum(
            "tf,df->td", grad_hidden, expand_full, preferred_element_type=jnp.float32
        )
        _, middle_pull = jax.vjp(layer_norm, normed, gain_one, shift_one)
        grad_one, grad_norm_gain, grad_norm_shift = middle_pull(grad_middle)
        grad_branch = grad_one.astype(jnp.bfloat16)
        grad_output_weight = jnp.einsum(
            "td,te->de", context, grad_branch, preferred_element_type=jnp.float32
        ).astype(jnp.bfloat16)
        return grad_one, grad_norm_gain, grad_norm_shift, grad_branch, grad_output_weight

    grad_one, grad_norm_gain, grad_norm_shift, grad_branch, grad_output_weight = ticks.tick(
        middle_back, (grad_hidden, grad_two, normed, context)
    )
    ticks.begin("grad_wide", reduce_chunk(links, [grad_expand_weight, grad_output_weight]))
    grad_output_bias = jnp.sum(grad_branch.astype(jnp.float32), axis=0)
    grad_context = jnp.einsum(
        "te,de->td", grad_branch, output_full, preferred_element_type=jnp.float32
    ).astype(jnp.bfloat16)
    parts = []
    joint_parts = []

    def joint_back(tokens, grad_joint):
        return jnp.einsum(
            "td,te->de", tokens, grad_joint, preferred_element_type=jnp.float32
        ).astype(jnp.bfloat16)

    for group in range(groups):

        def heads_back(queries, key_rows, values, grad_context, log_total, *before):
            grads = attend_backward(
                queries, key_rows, values, segment, log_total, grad_context, group_heads
            )
            grads = tuple(grad.astype(jnp.bfloat16) for grad in grads)
            return grads, [joint_back(tokens, grad_joint) for grad_joint in before]

        part, weight_grad = ticks.tick(
            heads_back,
            (
                columns_of(queries, group),
                columns_of(key_rows, group),
                columns_of(values, group),
                columns_of(grad_context, group),
                log_totals[group],
                *joint_parts[-1:],
            ),
        )
        if weight_grad:
            ticks.begin("grad_joint%d" % (group - 1), reduce_chunk(links, weight_grad))
        parts.append(part)
        joint_parts.append(jnp.concatenate(part, axis=1))
    grad_joint = jnp.concatenate(
        [parts[group][which] for which in range(3) for group in range(groups)], axis=1
    )
    grad_query_bias = jnp.sum(grad_joint[:, :model_width].astype(jnp.float32), axis=0)
    grad_value_bias = jnp.sum(grad_joint[:, 2 * model_width :].astype(jnp.float32), axis=0)
    weight_grad = ticks.tick(joint_back, (tokens, joint_parts[-1]))
    ticks.begin("grad_joint%d" % (groups - 1), reduce_chunk(links, [weight_grad]))
    vectors = [
        grad_query_bias,
        grad_value_bias,
        grad_output_bias,
        grad_norm_gain,
        grad_norm_shift,
        grad_expand_bias,
        grad_reduce_bias,
        grad_final_gain,
        grad_final_shift,
    ]
    ticks.begin("grad_small", sum_small(links, jnp.concatenate(vectors)))

    def tokens_back(grad_one, grad_joint):
        return (
            grad_one
            + jnp.einsum("te,de->td", grad_joint, joint_full, preferred_element_type=jnp.float32)
        ).astype(jnp.bfloat16)

    grad_tokens = ticks.tick(tokens_back, (grad_one, grad_joint))
    joint_names = ["grad_joint%d" % group for group in range(groups)]
    (sum_expand, sum_output), (sum_reduce,), summed, *joint_sums = ticks.finish(
        "grad_wide", "grad_reduce", "grad_small", *joint_names
    )
    sum_joint = jnp.concatenate(
        [columns_of(joint_sum, which) for which in range(3) for (joint_sum,) in joint_sums], axis=1
    )
    shard = lax.axis_index("shard")
    small_sums = []
    start = 0
    for vector in vectors:
        size = vector.shape[0] // links.shard_count
        small_sums.append(lax.dynamic_slice(summed, (start + shard * size,), (size,)))
        start += vector.shape[0]
    attn_grads = (sum_joint, *small_sums[:2], sum_output, *small_sums[2:5])
    ffn_grads = (sum_expand, small_sums[5], sum_reduce, *small_sums[6:])
    return (
        output.astype(jnp.bfloat16),
        grad_tokens,
        attn_grads[0],
        attn_grads[1],
        attn_grads[2],
        attn_grads[3],
        attn_grads[4],
        attn_grads[5],
        attn_grads[6],
        ffn_grads[0],
        ffn_grads[1],
        ffn_grads[2],
        ffn_grads[3],
        ffn_grads[4],
        ffn_grads[5],
    )


def solution(mesh):
    placed = (
        P(("rep", "shard"), None),
        P(("rep", "shard"), None),
        P(("rep", "shard"), None),
        P("shard", None),
        P("shard"),
        P("shard"),
        P("shard", None),
        P("shard"),
        P("shard"),
        P("shard"),
        P("shard", None),
        P("shard"),
        P("shard", None),
        P("shard"),
        P("shard"),
        P("shard"),
    )
    return jax.shard_map(
        functools.partial(on_device, Links(mesh)),
        mesh=mesh,
        in_specs=placed,
        out_specs=(
            P(("rep", "shard"), None),
            P(("rep", "shard"), None),
            P("shard", None),
            P("shard"),
            P("shard"),
            P("shard", None),
            P("shard"),
            P("shard"),
            P("shard"),
            P("shard", None),
            P("shard"),
            P("shard", None),
            P("shard"),
            P("shard"),
            P("shard"),
        ),
        check_vma=False,
    )
```
